128 devices in a mesh: row: 8 (over y_hi, x), col: 4 (over y_lo, core), depth: 4 (over z).
Axes of the slice: x: 4, y: 4 (y_hi: 2, y_lo: 2; y = y_hi * 2 + y_lo), z: 4, core: 2. Of those that a mesh axis runs over, the one named last changes fastest.
Arguments:
- activations: bfloat16 [2048, 16384], P('depth', ('row', 'col')), may hold values from -6 to 6
- gradients: bfloat16 [2048, 16384], P('depth', ('row', 'col')), may hold values from -6 to 6
- act_factor: bfloat16 [16384, 16384], P('row', ('col', 'depth')), may hold values from -1.5 to 1.5
- grad_factor: bfloat16 [16384, 16384], P('row', ('col', 'depth')), may hold values from -1.5 to 1.5
Outputs:
- act_update: bfloat16 [16384, 16384], P('row', ('col', 'depth'))
- grad_update: bfloat16 [16384, 16384], P('row', ('col', 'depth'))
The draws below stay inside these ranges and needn't reach their ends.
All inputs are finite; a program needn't handle non-finite values.
Results may differ from the reference program's by a relative error of at most 0.001.
Values may be sent and summed in bfloat16 or wider, within the bound.
No kernel may reach another device: no remote copies, remote signals or barrier semaphores. Data moves between devices by JAX's collectives and lax.ppermute only.
A program may use at most 128 MiB of HBM per device.

```python
import jax
import jax.numpy as jnp
from jax import lax

D = 16384
TOKENS = 2048
N_ROW = 8


def block_scale(key, shape, split, smallest, largest):
    level = 1.0
    for axis_at, parts in split:
        steps = jax.random.uniform(jax.random.fold_in(jax.random.fold_in(key, 6), axis_at), (parts,), jnp.float32, smallest / len(split), largest / len(split))
        level = level * jnp.repeat(jnp.exp(steps), shape[axis_at] // parts).reshape((-1,) + (1,) * (len(shape) - 1 - axis_at))
    return level


def gaussian(key, extent, spread, reach, cuts=(), held_as=jnp.bfloat16):
    loudness = block_scale(key, extent, cuts, -0.22, 0.18) if cuts else 1.0
    values = jax.random.normal(key, extent, jnp.float32) * spread * loudness
    return jnp.minimum(jnp.maximum(values, -reach), reach).astype(held_as)


def setup_inputs(seed: int = 0) -> dict:
    splits = jax.random.split(jax.random.key(seed), 5)
    activations = gaussian(splits[0], (TOKENS, D), 1.0, 6.0, ((0, 4), (1, 32)))
    gradients = gaussian(splits[1], (TOKENS, D), 1.0, 6.0, ((0, 4), (1, 32)))
    act_factor = gaussian(splits[2], (D, D), 0.25, 1.5, ((0, 8), (1, 16)))
    grad_factor = gaussian(splits[3], (D, D), 0.25, 1.5, ((0, 8), (1, 16)))
    return dict(activations=activations, gradients=gradients, act_factor=act_factor, grad_factor=grad_factor)


decay_rate = 0.5


def moving_average(previous, product, token_count):
    return (decay_rate * previous.astype(jnp.float32) + (1.0 - decay_rate) * (product / token_count)).astype(jnp.bfloat16)


def refresh(samples, previous):
    span_rows = D // N_ROW

    def one_block(position):
        row_block = lax.dynamic_slice_in_dim(samples, position * span_rows, span_rows, 1)
        product = jnp.dot(row_block.T, samples, preferred_element_type=jnp.float32)
        old_rows = lax.dynamic_slice_in_dim(previous, position * span_rows, span_rows, 0)
        return moving_average(old_rows, product, TOKENS)

    blocks = lax.map(one_block, jnp.arange(N_ROW, dtype=jnp.int32))
    return blocks.reshape(D, D)


def reference(activations, gradients, act_factor, grad_factor):
    return refresh(activations, act_factor), refresh(gradients, grad_factor)
```

```python
import functools

import jax
import jax.numpy as jnp
from jax import lax
from jax.experimental import pallas as pl
from jax.experimental.pallas import tpu as pltpu
from jax.sharding import Mesh, PartitionSpec as P

decay_rate = 0.5
AXES = ("yh", "x", "yl", "core", "z")
SIZES = (2, 4, 2, 2, 4)
PIECE = 512
ROW_TILE = 256


def index(yh, x, yl, core, z):
    return (((yh % 2 * 4 + x % 4) * 2 + yl % 2) * 2 + core % 2) * 4 + z % 4


def permutation(move):
    every = [
        (yh, x, yl, core, z)
        for yh in range(2)
        for x in range(4)
        for yl in range(2)
        for core in range(2)
        for z in range(4)
    ]
    return [(index(*place), index(*move(*place))) for place in every]


def scatter_move(yh, x, yl, core, z):
    depth = 2 * (x % 2) + yl
    return core, x + z - depth + 2 + 2 * core, yh, x // 2, depth


def y_move(yh, x, yl, core, z):
    y = (2 * yh + yl + 1 - 2 * core) % 4
    return y // 2, x, y % 2, core, z


SCATTER = permutation(scatter_move)
RING_X = permutation(lambda yh, x, yl, core, z: (yh, x + 1 - 2 * core, yl, core, z))
RING_Z = permutation(lambda yh, x, yl, core, z: (yh, x, yl, core, z + 1 - 2 * core))
RING_Y = permutation(y_move)
SWAP_YL = permutation(lambda yh, x, yl, core, z: (yh, x, 1 - yl, core, z))
SWAP_CORE = permutation(lambda yh, x, yl, core, z: (yh, x, yl, 1 - core, z))


def send(block, moves):
    return lax.ppermute(block, AXES, moves)


def update_kernel(tokens, place, *refs):
    left_refs, right_refs = refs[:8], refs[8:16]
    factor_ref, out_ref, left, right, left_sems, right_sems = refs[16:]
    yh, x, yl, core, z = (place[i] for i in range(5))
    step = pl.program_id(0)

    @pl.when(step == 0)
    def _():
        copies = []
        toward = 1 - 2 * core
        for s in range(4):
            for chain in range(2):
                source = lax.rem(x - s * toward + 4, 4)
                half = lax.rem(yh + chain, 2)
                token = lax.rem(source - 2 * core - z // 2 + z + 2 + 2 * half + 8, 4)
                copies.append(
                    pltpu.make_async_copy(
                        right_refs[4 * chain + s],
                        right.at[
                            pl.ds(pl.multiple_of(token * PIECE, PIECE), PIECE),
                            pl.ds(pl.multiple_of(half * PIECE, PIECE), PIECE),
                        ],
                        right_sems.at[4 * chain + s],
                    )
                )
        for s in range(4):
            for other in range(2):
                held_by = lax.rem(core + other, 2)
                token = lax.rem(z - s * (1 - 2 * held_by) + 4, 4)
                for partner in range(2):
                    block = 2 * lax.rem(yl + partner, 2) + held_by
                    copies.append(
                        pltpu.make_async_copy(
                            left_refs[4 * other + s].at[pl.ds(partner * PIECE, PIECE), :],
                            left.at[
                                pl.ds(pl.multiple_of(block * PIECE, PIECE), PIECE),
                                pl.ds(pl.multiple_of(token * PIECE, PIECE), PIECE),
                            ],
                            left_sems.at[8 * other + 2 * s + partner],
                        )
                    )
        for copy in copies:
            copy.start()
        for copy in copies:
            copy.wait()

    rows = pl.ds(pl.multiple_of(step * ROW_TILE, ROW_TILE), ROW_TILE)
    product = jnp.dot(left[rows, :], right[...], preferred_element_type=jnp.float32)
    out_ref[...] = (
        decay_rate * factor_ref[...].astype(jnp.float32)
        + (1.0 - decay_rate) * (product / tokens)
    ).astype(out_ref.dtype)


def update(place, lefts, rights, factor):
    rows, columns = factor.shape
    tokens = 4 * PIECE
    anywhere = pl.BlockSpec(memory_space=pl.ANY)
    tile = pl.BlockSpec((ROW_TILE, columns), lambda i, place: (i, 0))
    return pl.pallas_call(
        functools.partial(update_kernel, tokens),
        out_shape=jax.ShapeDtypeStruct((rows, columns), factor.dtype),
        grid_spec=pltpu.PrefetchScalarGridSpec(
            num_scalar_prefetch=1,
            grid=(rows // ROW_TILE,),
            in_specs=[anywhere] * 16 + [tile],
            out_specs=tile,
            scratch_shapes=[
                pltpu.VMEM((rows, tokens), jnp.bfloat16),
                pltpu.VMEM((tokens, columns), jnp.bfloat16),
                pltpu.SemaphoreType.DMA((16,)),
                pltpu.SemaphoreType.DMA((8,)),
            ],
        ),
        compiler_params=pltpu.CompilerParams(vmem_limit_bytes=28 * 2**20),
        cost_estimate=pl.CostEstimate(
            flops=2 * rows * columns * tokens,
            bytes_accessed=2 * (rows * tokens + tokens * columns + 2 * rows * columns),
            transcendentals=0,
        ),
    )(place, *lefts, *rights, factor)


def ring(block, moves):
    blocks = [block]
    for _ in range(3):
        blocks.append(send(blocks[-1], moves))
    return blocks


def refresh(place, samples, factor):
    scattered = send(samples, SCATTER)
    partner = send(samples, SWAP_YL)
    mine = ring(jnp.concatenate([samples.T, partner.T], axis=0), RING_Z)
    others = [send(block, SWAP_CORE) for block in mine]
    across = send(send(scattered, RING_Y), RING_Y)
    rights = ring(scattered, RING_X) + ring(across, RING_X)
    return update(place, mine + others, rights, factor)


def shards(activations, gradients, act_factor, grad_factor):
    place = jnp.stack([lax.axis_index(axis) for axis in AXES]).astype(jnp.int32)
    return (
        refresh(place, activations, act_factor),
        refresh(place, gradients, grad_factor),
    )


def solution(mesh):
    fine = Mesh(mesh.devices.reshape(SIZES), AXES)
    row, col, depth = ("yh", "x"), ("yl", "core"), "z"
    samples = P(depth, row + col)
    factor = P(row, col + (depth,))
    return jax.shard_map(
        shards,
        mesh=fine,
        in_specs=(samples, samples, factor, factor),
        out_specs=(factor, factor),
        check_vma=False,
    )
```

```python
import functools

import jax
import jax.numpy as jnp
from jax import lax
from jax.experimental import pallas as pl
from jax.experimental.pallas import tpu as pltpu
from jax.sharding import Mesh, PartitionSpec as P

decay_rate = 0.5
AXES = ("yh", "x", "yl", "core", "z")
SIZES = (2, 4, 2, 2, 4)
PIECE = 512


AT = (0, -1, -2, -3)


def index(yh, x, yl, core, z):
    return (((yh % 2 * 4 + x % 4) * 2 + yl % 2) * 2 + core % 2) * 4 + z % 4


def permutation(move):
    every = [
        (yh, x, yl, core, z)
        for yh in range(2)
        for x in range(4)
        for yl in range(2)
        for core in range(2)
        for z in range(4)
    ]
    return [(index(*place), index(*move(*place))) for place in every]


def along_x(yh, x, yl, core, z):
    return x + z - 2 * (x % 2) - yl + 2 + 2 * core


def scatter_move(yh, x, yl, core, z):
    return core, along_x(yh, x, yl, core, z), yh, x // 2, 2 * (x % 2) + yl


SCATTER = permutation(scatter_move)
BACK_X = permutation(lambda yh, x, yl, core, z: (yh, x - 1 + 2 * core, yl, core, z))
BACK_Z = permutation(lambda yh, x, yl, core, z: (yh, x, yl, core, z - 1 + 2 * core))
RING_X = permutation(lambda yh, x, yl, core, z: (yh, x + 1 - 2 * core, yl, core, z))
RING_Z = permutation(lambda yh, x, yl, core, z: (yh, x, yl, core, z + 1 - 2 * core))
ACROSS_Y = permutation(lambda yh, x, yl, core, z: (1 - yh, x, yl, core, z))
SWAP_YL = permutation(lambda yh, x, yl, core, z: (yh, x, 1 - yl, core, z))
SWAP_CORE = permutation(lambda yh, x, yl, core, z: (yh, x, yl, 1 - core, z))


def send(block, moves):
    return lax.ppermute(block, AXES, moves)


def update_kernel(tokens, factor_at, groups, halves, place, *refs):
    n_left, n_right = 4 * len(groups), 4 * len(halves)
    left_refs, right_refs = refs[:n_left], refs[n_left : n_left + n_right]
    factor_ref, out_ref, left, right, left_sems, right_sems = refs[-6:]
    yh, x, yl, core, z = (place[i] for i in range(5))
    step = pl.program_id(0)
    toward = 1 - 2 * core

    def right_copy(j, s):
        half = lax.rem(yh + halves[j], 2)
        source = x + AT[s] * toward
        token = source - 2 * core - z // 2 + z + 2 + 2 * half
        column = 0 if len(halves) == 1 else pl.multiple_of(half * PIECE, PIECE)
        row = pl.multiple_of(lax.rem(token + 8, 4) * PIECE, PIECE)
        return pltpu.make_async_copy(
            right_refs[4 * j + s],
            right.at[pl.ds(row, PIECE), pl.ds(column, PIECE)],
            right_sems.at[4 * j + s],
        )

    def left_copy(g, s):
        held_by = lax.rem(core + groups[g] // 2, 2)
        token = lax.rem(z + AT[s] * (1 - 2 * held_by) + 4, 4)
        return pltpu.make_async_copy(
            left_refs[4 * g + s].at[groups[g] % 2],
            left.at[g, pl.ds(pl.multiple_of(token * PIECE, PIECE), PIECE), :],
            left_sems.at[4 * g + s],
        )

    @pl.when(step == 0)
    def _():
        for s in range(4):
            for j in range(len(halves)):
                right_copy(j, s).start()
            left_copy(0, s).start()
        for s in range(4):
            for j in range(len(halves)):
                right_copy(j, s).wait()

    for g in range(len(groups)):

        @pl.when(step == g)
        def _():
            for s in range(4):
                left_copy(g, s).wait()
            if g + 1 < len(groups):
                for s in range(4):
                    left_copy(g + 1, s).start()

    product = lax.dot_general(
        left[step], right[...], (((0,), (0,)), ((), ())), preferred_element_type=jnp.float32
    )
    out_ref[...] = (
        decay_rate * factor_ref[...].astype(jnp.float32)
        + (1.0 - decay_rate) * (product / tokens)
    ).astype(out_ref.dtype)


def update(place, factor_at, groups, halves, lefts, rights, factor, out):
    rows, columns = factor.shape
    tokens = 4 * PIECE
    width = PIECE * len(halves)

    def block(step, place):
        group = groups[0] + step * (groups[1] - groups[0])
        row = 2 * lax.rem(place[2] + group % 2, 2) + lax.rem(place[3] + group // 2, 2)
        return row, 0 if len(halves) == 2 else lax.rem(place[0] + halves[0], 2)

    tile = pl.BlockSpec((PIECE, width), block)
    elsewhere = pl.BlockSpec(memory_space=pltpu.HBM)
    before = [] if out is None else [out]
    return pl.pallas_call(
        functools.partial(update_kernel, tokens, factor_at, groups, halves),
        out_shape=jax.ShapeDtypeStruct((rows, columns), factor.dtype),
        grid_spec=pltpu.PrefetchScalarGridSpec(
            num_scalar_prefetch=1,
            grid=(len(groups),),
            in_specs=[elsewhere] * (len(lefts) + len(rights) + len(before)) + [tile],
            out_specs=tile,
            scratch_shapes=[
                pltpu.VMEM((len(groups), tokens, PIECE), jnp.bfloat16),
                pltpu.VMEM((tokens, width), jnp.bfloat16),
                pltpu.SemaphoreType.DMA((len(lefts),)),
                pltpu.SemaphoreType.DMA((len(rights),)),
            ],
        ),
        input_output_aliases={1 + len(lefts) + len(rights): 0} if before else {},
        compiler_params=pltpu.CompilerParams(vmem_limit_bytes=60 * 2**20),
        cost_estimate=pl.CostEstimate(
            flops=1000,
            bytes_accessed=1000,
            transcendentals=0,
        ),
    )(place, *lefts, *rights, *before, factor)


def shards(activations, gradients, act_factor, grad_factor):
    place = jnp.stack([lax.axis_index(axis) for axis in AXES]).astype(jnp.int32)
    held = {"a": activations, "b": gradients, "fa": act_factor, "fb": grad_factor}

    def gated(name, gates):
        if not gates:
            return held[name]
        names = (name, *gates)
        held.update(zip(names, lax.optimization_barrier(tuple(held[n] for n in names))))
        return held[name]

    for name, source, how, gates in ORDER:
        if how == "join":
            held[name] = jnp.stack([held[source], gated(gates[0], ())])
        elif how in PARTS:
            f, groups, halves, before = PARTS[how]
            kinds = ["m", "m", "M", "M"]
            lefts = [held[f + kinds[g] + str(s)] for g in groups for s in range(4)]
            rights = [held[f + "rq"[j] + str(s)] for j in halves for s in range(4)]
            out = held["o" + f] if before else None
            held["o" + f] = update(place, f, groups, halves, lefts, rights, gated("f" + f, gates), out)
        else:
            held[name] = send(gated(source, gates), MOVES[how])
    return held["oa"], held["ob"]


PARTS = {
    "KA": ("a", (0, 1, 2, 3), (0, 1), False),
    "KB": ("b", (0, 1, 2, 3), (0, 1), False),
}
MOVES = {
    "z": RING_Z,
    "x": RING_X,
    "-z": BACK_Z,
    "-x": BACK_X,
    "y": ACROSS_Y,
    "l": SWAP_YL,
    "c": SWAP_CORE,
    "s": SCATTER,
}
ORDER = (
    ("ar0", "a", "s", ()),
    ("ar1", "ar0", "x", ()),
    ("aq0", "ar0", "y", ("ar1",)),
    ("ar2", "ar1", "x", ()),
    ("ar3", "ar2", "x", ()),
    ("aq1", "aq0", "x", ()),
    ("aq2", "aq1", "x", ()),
    ("aq3", "aq2", "x", ()),
    ("br0", "b", "s", ()),
    ("aY", "a", "l", ("br0",)),
    ("am0", "a", "join", ("aY",)),
    ("aM0", "am0", "c", ()),
    ("am1", "am0", "z", ()),
    ("am2", "am1", "z", ()),
    ("am3", "am2", "z", ()),
    ("aM1", "am1", "c", ()),
    ("aM2", "am2", "c", ()),
    ("aM3", "am3", "c", ()),
    ("bY", "b", "l", ()),
    ("bm0", "b", "join", ("bY",)),
    ("bM0", "bm0", "c", ()),
    ("bm1", "bm0", "z", ()),
    ("bm2", "bm1", "z", ()),
    ("bm3", "bm2", "z", ()),
    ("br1", "br0", "x", ()),
    ("bq0", "br0", "y", ("br1",)),
    ("br2", "br1", "x", ()),
    ("br3", "br2", "x", ()),
    ("bq1", "bq0", "x", ()),
    ("bq2", "bq1", "x", ()),
    ("bq3", "bq2", "x", ()),
    ("bM1", "bm1", "c", ()),
    ("bM2", "bm2", "c", ()),
    ("bM3", "bm3", "c", ()),
    ("KA", "x", "KA", ()),
    ("KB", "x", "KB", ()),
)


def solution(mesh):
    fine = Mesh(mesh.devices.reshape(SIZES), AXES)
    row, col, depth = ("yh", "x"), ("yl", "core"), "z"
    samples = P(depth, row + col)
    factor = P(row, col + (depth,))
    return jax.shard_map(
        shards,
        mesh=fine,
        in_specs=(samples, samples, factor, factor),
        out_specs=(factor, factor),
        check_vma=False,
    )
```

```python
import functools

import jax
import jax.numpy as jnp
from jax import lax
from jax.experimental import pallas as pl
from jax.experimental.pallas import tpu as pltpu
from jax.sharding import Mesh, PartitionSpec as P

decay_rate = 0.5
AXES = ("yh", "x", "yl", "core", "z")
SIZES = (2, 4, 2, 2, 4)
PIECE = 512


AT = (0, -1, -2, -3)


def index(yh, x, yl, core, z):
    return (((yh % 2 * 4 + x % 4) * 2 + yl % 2) * 2 + core % 2) * 4 + z % 4


def permutation(move):
    every = [
        (yh, x, yl, core, z)
        for yh in range(2)
        for x in range(4)
        for yl in range(2)
        for core in range(2)
        for z in range(4)
    ]
    return [(index(*place), index(*move(*place))) for place in every]


def along_x(yh, x, yl, core, z):
    return x + z - 2 * (x % 2) - yl + 2 + 2 * core


def scatter_move(yh, x, yl, core, z):
    return core, along_x(yh, x, yl, core, z), yh, x // 2, 2 * (x % 2) + yl


SCATTER = permutation(scatter_move)
BACK_X = permutation(lambda yh, x, yl, core, z: (yh, x - 1 + 2 * core, yl, core, z))
BACK_Z = permutation(lambda yh, x, yl, core, z: (yh, x, yl, core, z - 1 + 2 * core))
RING_X = permutation(lambda yh, x, yl, core, z: (yh, x + 1 - 2 * core, yl, core, z))
RING_Z = permutation(lambda yh, x, yl, core, z: (yh, x, yl, core, z + 1 - 2 * core))
ACROSS_Y = permutation(lambda yh, x, yl, core, z: (1 - yh, x, yl, core, z))
SWAP_YL = permutation(lambda yh, x, yl, core, z: (yh, x, 1 - yl, core, z))
SWAP_CORE = permutation(lambda yh, x, yl, core, z: (yh, x, yl, 1 - core, z))


def send(block, moves):
    return lax.ppermute(block, AXES, moves)


def update_kernel(tokens, factor_at, groups, halves, place, *refs):
    n_left, n_right = 4 * len(groups), 4 * len(halves)
    left_refs, right_refs = refs[:n_left], refs[n_left : n_left + n_right]
    factor_ref, out_ref, left, right, left_sems, right_sems = refs[-6:]
    yh, x, yl, core, z = (place[i] for i in range(5))
    step = pl.program_id(0)
    toward = 1 - 2 * core

    def right_copy(j, s):
        half = lax.rem(yh + halves[j], 2)
        source = x + AT[s] * toward
        token = source - 2 * core - z // 2 + z + 2 + 2 * half
        column = 0 if len(halves) == 1 else pl.multiple_of(half * PIECE, PIECE)
        row = pl.multiple_of(lax.rem(token + 8, 4) * PIECE, PIECE)
        return pltpu.make_async_copy(
            right_refs[4 * j + s],
            right.at[pl.ds(row, PIECE), pl.ds(column, PIECE)],
            right_sems.at[4 * j + s],
        )

    def left_copy(g, s):
        held_by = lax.rem(core + groups[g] // 2, 2)
        token = lax.rem(z + AT[s] * (1 - 2 * held_by) + 4, 4)
        return pltpu.make_async_copy(
            left_refs[4 * g + s].at[groups[g] % 2],
            left.at[g, pl.ds(pl.multiple_of(token * PIECE, PIECE), PIECE), :],
            left_sems.at[4 * g + s],
        )

    @pl.when(step == 0)
    def _():
        for s in range(4):
            for j in range(len(halves)):
                right_copy(j, s).start()
            left_copy(0, s).start()
        for s in range(4):
            for j in range(len(halves)):
                right_copy(j, s).wait()

    for g in range(len(groups)):

        @pl.when(step == g)
        def _():
            for s in range(4):
                left_copy(g, s).wait()
            if g + 1 < len(groups):
                for s in range(4):
                    left_copy(g + 1, s).start()

    product = lax.dot_general(
        left[step], right[...], (((0,), (0,)), ((), ())), preferred_element_type=jnp.float32
    )
    out_ref[...] = (
        decay_rate * factor_ref[...].astype(jnp.float32)
        + (1.0 - decay_rate) * (product / tokens)
    ).astype(out_ref.dtype)


def update(place, factor_at, groups, halves, lefts, rights, factor, out):
    rows, columns = factor.shape
    tokens = 4 * PIECE
    width = PIECE * len(halves)

    def block(step, place):
        group = groups[0] + step * (groups[1] - groups[0])
        row = 2 * lax.rem(place[2] + group % 2, 2) + lax.rem(place[3] + group // 2, 2)
        return row, 0 if len(halves) == 2 else lax.rem(place[0] + halves[0], 2)

    tile = pl.BlockSpec((PIECE, width), block)
    elsewhere = pl.BlockSpec(memory_space=pltpu.HBM)
    before = [] if out is None else [out]
    return pl.pallas_call(
        functools.partial(update_kernel, tokens, factor_at, groups, halves),
        out_shape=jax.ShapeDtypeStruct((rows, columns), factor.dtype),
        grid_spec=pltpu.PrefetchScalarGridSpec(
            num_scalar_prefetch=1,
            grid=(len(groups),),
            in_specs=[elsewhere] * (len(lefts) + len(rights) + len(before)) + [tile],
            out_specs=tile,
            scratch_shapes=[
                pltpu.VMEM((len(groups), tokens, PIECE), jnp.bfloat16),
                pltpu.VMEM((tokens, width), jnp.bfloat16),
                pltpu.SemaphoreType.DMA((len(lefts),)),
                pltpu.SemaphoreType.DMA((len(rights),)),
            ],
        ),
        input_output_aliases={1 + len(lefts) + len(rights): 0} if before else {},
        compiler_params=pltpu.CompilerParams(vmem_limit_bytes=60 * 2**20),
        cost_estimate=pl.CostEstimate(
            flops=1000,
            bytes_accessed=1000,
            transcendentals=0,
        ),
    )(place, *lefts, *rights, *before, factor)


def shards(activations, gradients, act_factor, grad_factor):
    place = jnp.stack([lax.axis_index(axis) for axis in AXES]).astype(jnp.int32)
    held = {"a": activations, "b": gradients, "fa": act_factor, "fb": grad_factor}

    def gated(name, gates):
        if not gates:
            return held[name]
        names = (name, *gates)
        held.update(zip(names, lax.optimization_barrier(tuple(held[n] for n in names))))
        return held[name]

    for name, source, how, gates in ORDER:
        if how == "join":
            held[name] = jnp.stack([held[source], gated(gates[0], ())])
        elif how in PARTS:
            f, groups, halves, before = PARTS[how]
            kinds = ["m", "m", "M", "M"]
            lefts = [held[f + kinds[g] + str(s)] for g in groups for s in range(4)]
            rights = [held[f + "rq"[j] + str(s)] for j in halves for s in range(4)]
            out = held["o" + f] if before else None
            held["o" + f] = update(place, f, groups, halves, lefts, rights, gated("f" + f, gates), out)
        else:
            held[name] = send(gated(source, gates), MOVES[how])
    return held["oa"], held["ob"]


PARTS = {
    "KA": ("a", (0, 1, 2, 3), (0, 1), False),
    "KB": ("b", (0, 1, 2, 3), (0, 1), False),
}
MOVES = {
    "z": RING_Z,
    "x": RING_X,
    "-z": BACK_Z,
    "-x": BACK_X,
    "y": ACROSS_Y,
    "l": SWAP_YL,
    "c": SWAP_CORE,
    "s": SCATTER,
}
ORDER = (
    ("ar0", "a", "s", ()),
    ("ar1", "ar0", "x", ()),
    ("aq0", "ar0", "y", ("ar1",)),
    ("ar2", "ar1", "x", ()),
    ("ar3", "ar2", "x", ()),
    ("aq1", "aq0", "x", ()),
    ("aq2", "aq1", "x", ()),
    ("aq3", "aq2", "x", ()),
    ("br0", "b", "s", ()),
    ("aY", "a", "l", ("br0",)),
    ("am0", "a", "join", ("aY",)),
    ("aM0", "am0", "c", ()),
    ("am1", "am0", "z", ()),
    ("am2", "am1", "z", ()),
    ("am3", "am2", "z", ()),
    ("aM1", "am1", "c", ()),
    ("aM2", "am2", "c", ()),
    ("aM3", "am3", "c", ()),
    ("bY", "b", "l", ()),
    ("bm0", "b", "join", ("bY",)),
    ("bM0", "bm0", "c", ()),
    ("bm1", "bm0", "z", ()),
    ("bm2", "bm1", "z", ()),
    ("bm3", "bm2", "z", ()),
    ("br1", "br0", "x", ()),
    ("br2", "br1", "x", ()),
    ("bq0", "br0", "y", ("br2",)),
    ("br3", "br2", "x", ()),
    ("bq1", "bq0", "x", ()),
    ("bq2", "bq1", "x", ()),
    ("bq3", "br3", "y", ()),
    ("bM1", "bm1", "c", ()),
    ("bM2", "bm2", "c", ()),
    ("bM3", "bm3", "c", ()),
    ("KA", "x", "KA", ()),
    ("KB", "x", "KB", ()),
)


def solution(mesh):
    fine = Mesh(mesh.devices.reshape(SIZES), AXES)
    row, col, depth = ("yh", "x"), ("yl", "core"), "z"
    samples = P(depth, row + col)
    factor = P(row, col + (depth,))
    return jax.shard_map(
        shards,
        mesh=fine,
        in_specs=(samples, samples, factor, factor),
        out_specs=(factor, factor),
        check_vma=False,
    )
```

```python
import functools

import jax
import jax.numpy as jnp
from jax import lax
from jax.experimental import pallas as pl
from jax.experimental.pallas import tpu as pltpu
from jax.sharding import Mesh, PartitionSpec as P

decay_rate = 0.5
AXES = ("yh", "x", "yl", "core", "z")
SIZES = (2, 4, 2, 2, 4)
PIECE = 512


AT = (0, -1, -2, -3)


def index(yh, x, yl, core, z):
    return (((yh % 2 * 4 + x % 4) * 2 + yl % 2) * 2 + core % 2) * 4 + z % 4


def permutation(move):
    every = [
        (yh, x, yl, core, z)
        for yh in range(2)
        for x in range(4)
        for yl in range(2)
        for core in range(2)
        for z in range(4)
    ]
    return [(index(*place), index(*move(*place))) for place in every]


def along_x(yh, x, yl, core, z):
    return x + z - 2 * (x % 2) - yl + 2


def scatter_move(yh, x, yl, core, z):
    return core + yl, along_x(yh, x, yl, core, z), yh, x // 2, 2 * (x % 2) + yl


SCATTER = permutation(scatter_move)
BACK_X = permutation(lambda yh, x, yl, core, z: (yh, x - 1 + 2 * core, yl, core, z))
BACK_Z = permutation(lambda yh, x, yl, core, z: (yh, x, yl, core, z - 1 + 2 * core))
RING_X = permutation(lambda yh, x, yl, core, z: (yh, x + 1 - 2 * core, yl, core, z))
RING_Z = permutation(lambda yh, x, yl, core, z: (yh, x, yl, core, z + 1 - 2 * core))
ACROSS_Y = permutation(lambda yh, x, yl, core, z: (1 - yh, x, yl, core, z))
SWAP_YL = permutation(lambda yh, x, yl, core, z: (yh, x, 1 - yl, core, z))
SWAP_CORE = permutation(lambda yh, x, yl, core, z: (yh, x, yl, 1 - core, z))


def send(block, moves):
    return lax.ppermute(block, AXES, moves)


def update_kernel(tokens, factor_at, groups, halves, place, *refs):
    n_left, n_right = 4 * len(groups), 4 * len(halves)
    left_refs, right_refs = refs[:n_left], refs[n_left : n_left + n_right]
    factor_ref, out_ref, left, right, left_sems, right_sems = refs[-6:]
    yh, x, yl, core, z = (place[i] for i in range(5))
    step = pl.program_id(0)
    toward = 1 - 2 * core

    def right_copy(j, s):
        half = lax.rem(yh + halves[j] + z, 2)
        source = x + AT[s] * toward
        token = source - 2 * core - z // 2 + z + 2
        column = 0 if len(halves) == 1 else pl.multiple_of(half * PIECE, PIECE)
        row = pl.multiple_of(lax.rem(token + 8, 4) * PIECE, PIECE)
        return pltpu.make_async_copy(
            right_refs[4 * j + s],
            right.at[pl.ds(row, PIECE), pl.ds(column, PIECE)],
            right_sems.at[4 * j + s],
        )

    def left_copy(g, s):
        held_by = lax.rem(core + groups[g] // 2, 2)
        token = lax.rem(z + AT[s] * (1 - 2 * held_by) + 4, 4)
        return pltpu.make_async_copy(
            left_refs[4 * g + s].at[groups[g] % 2],
            left.at[g, pl.ds(pl.multiple_of(token * PIECE, PIECE), PIECE), :],
            left_sems.at[4 * g + s],
        )

    @pl.when(step == 0)
    def _():
        for s in range(4):
            for j in range(len(halves)):
                right_copy(j, s).start()
            left_copy(0, s).start()
        for s in range(4):
            for j in range(len(halves)):
                right_copy(j, s).wait()

    for g in range(len(groups)):

        @pl.when(step == g)
        def _():
            for s in range(4):
                left_copy(g, s).wait()
            if g + 1 < len(groups):
                for s in range(4):
                    left_copy(g + 1, s).start()

    product = lax.dot_general(
        left[step], right[...], (((0,), (0,)), ((), ())), preferred_element_type=jnp.float32
    )
    out_ref[...] = (
        decay_rate * factor_ref[...].astype(jnp.float32)
        + (1.0 - decay_rate) * (product / tokens)
    ).astype(out_ref.dtype)


def update(place, factor_at, groups, halves, lefts, rights, factor, out):
    rows, columns = factor.shape
    tokens = 4 * PIECE
    width = PIECE * len(halves)

    def block(step, place):
        group = groups[0] + step * (groups[1] - groups[0])
        row = 2 * lax.rem(place[2] + group % 2, 2) + lax.rem(place[3] + group // 2, 2)
        return row, 0 if len(halves) == 2 else lax.rem(place[0] + halves[0] + place[4], 2)

    tile = pl.BlockSpec((PIECE, width), block)
    elsewhere = pl.BlockSpec(memory_space=pltpu.HBM)
    before = [] if out is None else [out]
    return pl.pallas_call(
        functools.partial(update_kernel, tokens, factor_at, groups, halves),
        out_shape=jax.ShapeDtypeStruct((rows, columns), factor.dtype),
        grid_spec=pltpu.PrefetchScalarGridSpec(
            num_scalar_prefetch=1,
            grid=(len(groups),),
            in_specs=[elsewhere] * (len(lefts) + len(rights) + len(before)) + [tile],
            out_specs=tile,
            scratch_shapes=[
                pltpu.VMEM((len(groups), tokens, PIECE), jnp.bfloat16),
                pltpu.VMEM((tokens, width), jnp.bfloat16),
                pltpu.SemaphoreType.DMA((len(lefts),)),
                pltpu.SemaphoreType.DMA((len(rights),)),
            ],
        ),
        input_output_aliases={1 + len(lefts) + len(rights): 0} if before else {},
        compiler_params=pltpu.CompilerParams(vmem_limit_bytes=60 * 2**20),
        cost_estimate=pl.CostEstimate(
            flops=1000,
            bytes_accessed=1000,
            transcendentals=0,
        ),
    )(place, *lefts, *rights, *before, factor)


def shards(activations, gradients, act_factor, grad_factor):
    place = jnp.stack([lax.axis_index(axis) for axis in AXES]).astype(jnp.int32)
    held = {"a": activations, "b": gradients, "fa": act_factor, "fb": grad_factor}

    def gated(name, gates):
        if not gates:
            return held[name]
        names = (name, *gates)
        held.update(zip(names, lax.optimization_barrier(tuple(held[n] for n in names))))
        return held[name]

    for name, source, how, gates in ORDER:
        if how == "join":
            held[name] = jnp.stack([held[source], gated(gates[0], ())])
        elif how in PARTS:
            f, groups, halves, before = PARTS[how]
            kinds = ["m", "m", "M", "M"]
            lefts = [held[f + kinds[g] + str(s)] for g in groups for s in range(4)]
            rights = [held[f + "rq"[j] + str(s)] for j in halves for s in range(4)]
            out = held["o" + f] if before else None
            held["o" + f] = update(place, f, groups, halves, lefts, rights, gated("f" + f, gates), out)
        else:
            held[name] = send(gated(source, gates), MOVES[how])
    return held["oa"], held["ob"]


PARTS = {
    "KA": ("a", (0, 1, 2, 3), (0, 1), False),
    "KB": ("b", (0, 1, 2, 3), (0, 1), False),
}
MOVES = {
    "z": RING_Z,
    "x": RING_X,
    "-z": BACK_Z,
    "-x": BACK_X,
    "y": ACROSS_Y,
    "l": SWAP_YL,
    "c": SWAP_CORE,
    "s": SCATTER,
}
ORDER = (
    ("ar0", "a", "s", ()),
    ("ar1", "ar0", "x", ()),
    ("aq0", "ar0", "y", ("ar1",)),
    ("ar2", "ar1", "x", ()),
    ("ar3", "ar2", "x", ()),
    ("aq1", "aq0", "x", ()),
    ("aq2", "aq1", "x", ()),
    ("aq3", "aq2", "x", ()),
    ("br0", "b", "s", ()),
    ("aY", "a", "l", ("br0",)),
    ("am0", "a", "join", ("aY",)),
    ("aM0", "am0", "c", ()),
    ("am1", "am0", "z", ()),
    ("am2", "am1", "z", ()),
    ("am3", "am2", "z", ()),
    ("aM1", "am1", "c", ()),
    ("aM2", "am2", "c", ()),
    ("aM3", "am3", "c", ()),
    ("bY", "b", "l", ()),
    ("bm0", "b", "join", ("bY",)),
    ("bM0", "bm0", "c", ()),
    ("bm1", "bm0", "z", ()),
    ("bm2", "bm1", "z", ()),
    ("bm3", "bm2", "z", ()),
    ("br1", "br0", "x", ()),
    ("br2", "br1", "x", ()),
    ("bq0", "br0", "y", ("br2",)),
    ("br3", "br2", "x", ()),
    ("bq1", "bq0", "x", ()),
    ("bq2", "bq1", "x", ()),
    ("bq3", "br3", "y", ()),
    ("bM1", "bm1", "c", ()),
    ("bM2", "bm2", "c", ()),
    ("bM3", "bm3", "c", ()),
    ("KA", "x", "KA", ()),
    ("KB", "x", "KB", ()),
)


def solution(mesh):
    fine = Mesh(mesh.devices.reshape(SIZES), AXES)
    row, col, depth = ("yh", "x"), ("yl", "core"), "z"
    samples = P(depth, row + col)
    factor = P(row, col + (depth,))
    return jax.shard_map(
        shards,
        mesh=fine,
        in_specs=(samples, samples, factor, factor),
        out_specs=(factor, factor),
        check_vma=False,
    )
```

```python
import functools

import jax
import jax.numpy as jnp
from jax import lax
from jax.experimental import pallas as pl
from jax.experimental.pallas import tpu as pltpu
from jax.sharding import Mesh, PartitionSpec as P

decay_rate = 0.5
AXES = ("yh", "x", "yl", "core", "z")
SIZES = (2, 4, 2, 2, 4)
PIECE = 512


AT = (0, -1, -2, -3)


def index(yh, x, yl, core, z):
    return (((yh % 2 * 4 + x % 4) * 2 + yl % 2) * 2 + core % 2) * 4 + z % 4


def permutation(move):
    every = [
        (yh, x, yl, core, z)
        for yh in range(2)
        for x in range(4)
        for yl in range(2)
        for core in range(2)
        for z in range(4)
    ]
    return [(index(*place), index(*move(*place))) for place in every]


def along_x(yh, x, yl, core, z):
    return x + z - 2 * (x % 2) - yl + 2


def scatter_move(yh, x, yl, core, z):
    return core + yl, along_x(yh, x, yl, core, z), yh, x // 2, 2 * (x % 2) + yl


SCATTER = permutation(scatter_move)
BACK_X = permutation(lambda yh, x, yl, core, z: (yh, x - 1 + 2 * core, yl, core, z))
BACK_Z = permutation(lambda yh, x, yl, core, z: (yh, x, yl, core, z - 1 + 2 * core))
RING_X = permutation(lambda yh, x, yl, core, z: (yh, x + 1 - 2 * core, yl, core, z))
RING_Z = permutation(lambda yh, x, yl, core, z: (yh, x, yl, core, z + 1 - 2 * core))
ACROSS_Y = permutation(lambda yh, x, yl, core, z: (1 - yh, x, yl, core, z))
SWAP_YL = permutation(lambda yh, x, yl, core, z: (yh, x, 1 - yl, core, z))
SWAP_CORE = permutation(lambda yh, x, yl, core, z: (yh, x, yl, 1 - core, z))


def send(block, moves):
    return lax.ppermute(block, AXES, moves)


def update_kernel(tokens, factor_at, groups, halves, place, *refs):
    n_left, n_right = 4 * len(groups), 4 * len(halves)
    left_refs, right_refs = refs[:n_left], refs[n_left : n_left + n_right]
    factor_ref, out_ref, left, right, left_sems, right_sems = refs[-6:]
    yh, x, yl, core, z = (place[i] for i in range(5))
    step = pl.program_id(0)
    toward = 1 - 2 * core

    def right_copy(j, s):
        half = lax.rem(yh + halves[j] + z, 2)
        source = x + AT[s] * toward
        token = source - 2 * core - z // 2 + z + 2
        column = 0 if len(halves) == 1 else pl.multiple_of(half * PIECE, PIECE)
        row = pl.multiple_of(lax.rem(token + 8, 4) * PIECE, PIECE)
        return pltpu.make_async_copy(
            right_refs[4 * j + s],
            right.at[pl.ds(row, PIECE), pl.ds(column, PIECE)],
            right_sems.at[4 * j + s],
        )

    def left_copy(g, s):
        held_by = lax.rem(core + groups[g] // 2, 2)
        token = lax.rem(z + AT[s] * (1 - 2 * held_by) + 4, 4)
        return pltpu.make_async_copy(
            left_refs[4 * g + s].at[groups[g] % 2],
            left.at[g, pl.ds(pl.multiple_of(token * PIECE, PIECE), PIECE), :],
            left_sems.at[4 * g + s],
        )

    @pl.when(step == 0)
    def _():
        for s in range(4):
            for j in range(len(halves)):
                right_copy(j, s).start()
            left_copy(0, s).start()
        for s in range(4):
            for j in range(len(halves)):
                right_copy(j, s).wait()

    for g in range(len(groups)):

        @pl.when(step == g)
        def _():
            for s in range(4):
                left_copy(g, s).wait()
            if g + 1 < len(groups):
                for s in range(4):
                    left_copy(g + 1, s).start()

    product = lax.dot_general(
        left[step], right[...], (((0,), (0,)), ((), ())), preferred_element_type=jnp.float32
    )
    out_ref[...] = (
        decay_rate * factor_ref[...].astype(jnp.float32)
        + ((1.0 - decay_rate) / tokens) * product
    ).astype(out_ref.dtype)


def update(place, factor_at, groups, halves, lefts, rights, factor, out):
    rows, columns = factor.shape
    tokens = 4 * PIECE
    width = PIECE * len(halves)

    def block(step, place):
        group = groups[0] + step * (groups[1] - groups[0])
        row = 2 * lax.rem(place[2] + group % 2, 2) + lax.rem(place[3] + group // 2, 2)
        return row, 0 if len(halves) == 2 else lax.rem(place[0] + halves[0] + place[4], 2)

    tile = pl.BlockSpec((PIECE, width), block)
    elsewhere = pl.BlockSpec(memory_space=pltpu.HBM)
    before = [] if out is None else [out]
    return pl.pallas_call(
        functools.partial(update_kernel, tokens, factor_at, groups, halves),
        out_shape=jax.ShapeDtypeStruct((rows, columns), factor.dtype),
        grid_spec=pltpu.PrefetchScalarGridSpec(
            num_scalar_prefetch=1,
            grid=(len(groups),),
            in_specs=[elsewhere] * (len(lefts) + len(rights) + len(before)) + [tile],
            out_specs=tile,
            scratch_shapes=[
                pltpu.VMEM((len(groups), tokens, PIECE), jnp.bfloat16),
                pltpu.VMEM((tokens, width), jnp.bfloat16),
                pltpu.SemaphoreType.DMA((len(lefts),)),
                pltpu.SemaphoreType.DMA((len(rights),)),
            ],
        ),
        input_output_aliases={1 + len(lefts) + len(rights): 0} if before else {},
        compiler_params=pltpu.CompilerParams(vmem_limit_bytes=60 * 2**20),
        cost_estimate=pl.CostEstimate(
            flops=1000,
            bytes_accessed=1000,
            transcendentals=0,
        ),
    )(place, *lefts, *rights, *before, factor)


def shards(activations, gradients, act_factor, grad_factor):
    place = jnp.stack([lax.axis_index(axis) for axis in AXES]).astype(jnp.int32)
    held = {"a": activations, "b": gradients, "fa": act_factor, "fb": grad_factor}

    def gated(name, gates):
        if not gates:
            return held[name]
        names = (name, *gates)
        held.update(zip(names, lax.optimization_barrier(tuple(held[n] for n in names))))
        return held[name]

    for name, source, how, gates in ORDER:
        if how == "join":
            held[name] = jnp.stack([held[source], gated(gates[0], ())])
        elif how in PARTS:
            f, groups, halves, before = PARTS[how]
            kinds = ["m", "m", "M", "M"]
            lefts = [held[f + kinds[g] + str(s)] for g in groups for s in range(4)]
            rights = [held[f + "rq"[j] + str(s)] for j in halves for s in range(4)]
            out = held["o" + f] if before else None
            held["o" + f] = update(place, f, groups, halves, lefts, rights, gated("f" + f, gates), out)
        else:
            held[name] = send(gated(source, gates), MOVES[how])
    return held["oa"], held["ob"]


PARTS = {
    "KA": ("a", (0, 1, 2, 3), (0, 1), False),
    "KB": ("b", (0, 1, 2, 3), (0, 1), False),
}
MOVES = {
    "z": RING_Z,
    "x": RING_X,
    "-z": BACK_Z,
    "-x": BACK_X,
    "y": ACROSS_Y,
    "l": SWAP_YL,
    "c": SWAP_CORE,
    "s": SCATTER,
}
ORDER = (
    ("ar0", "a", "s", ()),
    ("ar1", "ar0", "x", ()),
    ("aq0", "ar0", "y", ("ar1",)),
    ("ar2", "ar1", "x", ()),
    ("ar3", "ar2", "x", ()),
    ("aq1", "aq0", "x", ()),
    ("aq2", "aq1", "x", ()),
    ("aq3", "aq2", "x", ()),
    ("br0", "b", "s", ()),
    ("aY", "a", "l", ("br0",)),
    ("am0", "a", "join", ("aY",)),
    ("aM0", "am0", "c", ()),
    ("am1", "am0", "z", ()),
    ("am2", "am1", "z", ()),
    ("am3", "am2", "z", ()),
    ("aM1", "am1", "c", ()),
    ("aM2", "am2", "c", ()),
    ("aM3", "am3", "c", ()),
    ("bY", "b", "l", ()),
    ("bm0", "b", "join", ("bY",)),
    ("bM0", "bm0", "c", ()),
    ("bm1", "bm0", "z", ()),
    ("bm2", "bm1", "z", ()),
    ("bm3", "bm2", "z", ()),
    ("br1", "br0", "x", ()),
    ("br2", "br1", "x", ()),
    ("bq0", "br0", "y", ("br2",)),
    ("br3", "br2", "x", ()),
    ("bq1", "bq0", "x", ()),
    ("bq2", "bq1", "x", ()),
    ("bq3", "br3", "y", ()),
    ("bM1", "bm1", "c", ()),
    ("bM2", "bm2", "c", ()),
    ("bM3", "bm3", "c", ()),
    ("KA", "x", "KA", ()),
    ("KB", "x", "KB", ()),
)


def solution(mesh):
    fine = Mesh(mesh.devices.reshape(SIZES), AXES)
    row, col, depth = ("yh", "x"), ("yl", "core"), "z"
    samples = P(depth, row + col)
    factor = P(row, col + (depth,))
    return jax.shard_map(
        shards,
        mesh=fine,
        in_specs=(samples, samples, factor, factor),
        out_specs=(factor, factor),
        check_vma=False,
    )
```
